768 devices in a mesh: theta: 96 (over y_lo, z, x), axial: 8 (over y_hi, core).
Axes of the slice: x: 4, y: 8 (y_hi: 4, y_lo: 2; y = y_hi * 2 + y_lo), z: 12, core: 2. Of those that a mesh axis runs over, the one named last changes fastest.
Arguments:
- conserved: float32 [5, 1536, 128, 128], P(None, 'theta', 'axial'), may hold values from -6 to 6
- flux_matrices: float32 [3, 5, 5], replicated, may hold values from -2.5 to 2.5
- slide_weights: float32 [3, 2, 16, 16], replicated, may hold values from -1.5 to 1.5
- rotor_offsets: int32 [3], replicated, may hold values from 0 to 95
Outputs:
- advanced: float32 [5, 1536, 128, 128], P(None, 'theta', 'axial')
The draws below stay inside these ranges and needn't reach their ends.
All inputs are finite; a program needn't handle non-finite values.
Results may differ from the reference program's by a relative error of at most 0.00005.
Values sent between devices are 32-bit elements; how exact they have to be, the bound alone decides.
No kernel may reach another device: no remote copies, remote signals or barrier semaphores. Data moves between devices by JAX's collectives and lax.ppermute only.
A program may use at most 32 MiB of HBM per device.

```python
import jax
import jax.numpy as jnp
from jax import lax

NVAR = 5
SECTIONS = 3
CT = 16
CA = 16
RAD = 128
NTH = 1536
NAX = 128
N_THETA = 96
N_AXIAL = 8


def level_of(key, dims, cuts, low, largest):
    loudness = 1.0
    for axis_at, shards_of in cuts:
        draws = jax.random.uniform(jax.random.fold_in(jax.random.fold_in(key, 6), axis_at), (shards_of,), jnp.float32, low / len(cuts), largest / len(cuts))
        loudness = loudness * jnp.repeat(jnp.exp(draws), dims[axis_at] // shards_of).reshape((-1,) + (1,) * (len(dims) - 1 - axis_at))
    return loudness


def centred(rng, dims, deviation, most, split=(), kind=jnp.bfloat16):
    result = deviation * jax.random.normal(rng, dims, jnp.float32)
    if split:
        result = result * level_of(rng, dims, split, -0.22, 0.18)
    return jnp.clip(result, -most, most).astype(kind)


def setup_inputs(seed: int = 0) -> dict:
    key_of = jax.random.split(jax.random.key(seed), 5)
    return {
        "conserved": centred(key_of[0], (NVAR, NTH, NAX, RAD), 1.0, 6.0, ((1, 96), (2, 8)), jnp.float32),
        "flux_matrices": centred(key_of[1], (3, NVAR, NVAR), NVAR ** -0.5, 2.5, (), jnp.float32),
        "slide_weights": centred(key_of[2], (SECTIONS, 2, CT, CT), CT ** -0.5, 1.5, (), jnp.float32),
        "rotor_offsets": jax.random.randint(key_of[3], (SECTIONS,), 0, N_THETA).astype(jnp.int32),
    }


time_step = 0.25
viscosity = 0.3


def apply_matrix(matrix, values):
    return jnp.einsum('vw,wtar->vtar', matrix, values, precision=lax.Precision.HIGHEST)


def tendency(current, theta_plus, theta_minus, axial_plus, axial_minus, flux_matrices):
    radial_plus = jnp.concatenate([current[..., 1:], current[..., -1:]], axis=3)
    radial_minus = jnp.concatenate([current[..., :1], current[..., :-1]], axis=3)
    transport = apply_matrix(flux_matrices[0], 0.5 * (theta_plus - theta_minus))
    transport = transport + apply_matrix(flux_matrices[1], 0.5 * (axial_plus - axial_minus))
    transport = transport + apply_matrix(flux_matrices[2], 0.5 * (radial_plus - radial_minus))
    diffusion = theta_plus + theta_minus + axial_plus + axial_minus + radial_plus + radial_minus - 6.0 * current
    return viscosity * diffusion - transport


def rotate_sectors(face, shift_by, matrix):
    blocks_view = face.reshape(face.shape[0], N_THETA, CT, face.shape[-1])
    blocks_view = jnp.roll(blocks_view, shift_by, axis=1)
    mixed = jnp.einsum('cd,vsdr->vscr', matrix, blocks_view, precision=lax.Precision.HIGHEST)
    return mixed.reshape(face.shape)


def evaluate(current, section_index, flux_matrices, slide_weights, rotor_offsets):
    half_cells = CA * (N_AXIAL // 2)
    theta_plus = jnp.roll(current, -1, axis=1)
    theta_minus = jnp.roll(current, 1, axis=1)
    offset = rotor_offsets[section_index]
    from_rotor = rotate_sectors(current[:, :, half_cells - 1], offset, slide_weights[section_index, 0])
    from_stator = rotate_sectors(current[:, :, half_cells], -offset, slide_weights[section_index, 1])
    axial_plus = jnp.concatenate([current[:, :, 1:], current[:, :, -1:]], axis=2)
    axial_plus = axial_plus.at[:, :, half_cells - 1].set(from_stator)
    axial_minus = jnp.concatenate([current[:, :, :1], current[:, :, :-1]], axis=2)
    axial_minus = axial_minus.at[:, :, half_cells].set(from_rotor)
    return tendency(current, theta_plus, theta_minus, axial_plus, axial_minus, flux_matrices)


def reference(conserved, flux_matrices, slide_weights, rotor_offsets):
    first = conserved + time_step * evaluate(conserved, 0, flux_matrices, slide_weights, rotor_offsets)
    second = 0.75 * conserved + 0.25 * (first + time_step * evaluate(first, 1, flux_matrices, slide_weights, rotor_offsets))
    third = second + time_step * evaluate(second, 2, flux_matrices, slide_weights, rotor_offsets)
    return (1.0 / 3.0) * conserved + (2.0 / 3.0) * third
```

```python
import functools

import jax
import jax.numpy as jnp
from jax import lax
from jax.experimental import pallas as pl
from jax.experimental.pallas import tpu as pltpu
from jax.sharding import PartitionSpec as P

NVAR = 5
time_step = 0.25
viscosity = 0.3
SECTION_WEIGHTS = (
    (0.0, 1.0, time_step),
    (0.75, 0.25, 0.25 * time_step),
    (1.0 / 3.0, 2.0 / 3.0, 2.0 / 3.0 * time_step),
)
AXES = ("theta", "axial")
VMEM = pl.BlockSpec(memory_space=pltpu.VMEM)
SMEM = pl.BlockSpec(memory_space=pltpu.SMEM)


def write_rims(value_of, is_odd, theta_low, theta_high, core_rim, hop_rim, cells):
    for v in range(NVAR):
        theta_low[v] = value_of(v, 0)
        theta_high[v] = value_of(v, cells - 1)

    def step(t, carry):
        for v in range(NVAR):
            write_axial_rims(value_of(v, t), v, t, is_odd, core_rim, hop_rim)
        return carry

    lax.fori_loop(0, cells, step, 0)


def write_axial_rims(value, v, t, is_odd, core_rim, hop_rim):
    first, last = value[:1], value[-1:]
    core_rim[v, pl.ds(t, 1), :] = jnp.where(is_odd, first, last)
    hop_rim[v, pl.ds(t, 1), :] = jnp.where(is_odd, last, first)


def rims_kernel(place, current, theta_low, theta_high, core_rim, hop_rim):
    is_odd = place[0] % 2 == 1
    cells = current.shape[1]
    write_rims(
        lambda v, t: current[v, t], is_odd, theta_low, theta_high, core_rim, hop_rim, cells
    )


def section_kernel(section, blocks, last, *refs):
    place, flux, weights, current, conserved, before, after, core_in, hop_in, hop_own = refs[:10]
    rims = refs[11:-2]
    out, low_ghost, high_ghost = refs[10], refs[-2], refs[-1]
    index = place[0]
    is_odd = index % 2 == 1
    cells, width, radial = current.shape[1:]
    at_plane = (index == blocks // 2) | (index == blocks // 2 - 1)
    at_end = (index == 0) | (index == blocks - 1)
    inside = jnp.logical_not(at_plane | at_end)

    def put(core_side, hop_side):
        @pl.when(at_plane)
        def _():
            mix = weights[section, jnp.where(index == blocks // 2, 0, 1)]
            for v in range(NVAR):
                hop_side[v] = jnp.dot(
                    mix,
                    hop_in[v],
                    precision=lax.Precision.HIGHEST,
                    preferred_element_type=jnp.float32,
                )

        @pl.when(at_end)
        def _():
            hop_side[...] = hop_own[...]

        @pl.when(inside)
        def _():
            hop_side[...] = hop_in[...]

        core_side[...] = core_in[...]

    @pl.when(is_odd)
    def _():
        put(low_ghost, high_ghost)

    @pl.when(jnp.logical_not(is_odd))
    def _():
        put(high_ghost, low_ghost)

    keep, carry_on, push = SECTION_WEIGHTS[section]
    row = lax.broadcasted_iota(jnp.int32, (width, radial), 0)
    lane = lax.broadcasted_iota(jnp.int32, (width, radial), 1)

    def cell_row(t, minus_of, plus_of):
        slope = [None] * NVAR
        smooth = [None] * NVAR
        for w in range(NVAR):
            c = current[w, t]
            tm, tp = minus_of(w), plus_of(w)
            low = low_ghost[w, pl.ds(t, 1), :]
            high = high_ghost[w, pl.ds(t, 1), :]
            am = jnp.where(row == 0, low, pltpu.roll(c, 1, 0))
            ap = jnp.where(row == width - 1, high, pltpu.roll(c, width - 1, 0))
            rm = jnp.where(lane == 0, c, pltpu.roll(c, 1, 1))
            rp = jnp.where(lane == radial - 1, c, pltpu.roll(c, radial - 1, 1))
            total = (tm + tp) + (am + ap) + (rm + rp)
            smooth[w] = (viscosity * push) * total + (carry_on - 6.0 * viscosity * push) * c
            if section:
                smooth[w] = smooth[w] + keep * conserved[w, t]
            dt, da, dr = tp - tm, ap - am, rp - rm
            for v in range(NVAR):
                term = flux[0, v, w] * dt + flux[1, v, w] * da + flux[2, v, w] * dr
                slope[v] = term if slope[v] is None else slope[v] + term
        for v in range(NVAR):
            new = smooth[v] - (0.5 * push) * slope[v]
            out[v, t] = new
            if not last:
                write_axial_rims(new, v, t, is_odd, rims[2], rims[3])

    def step(t, carry):
        cell_row(t, lambda w: current[w, t - 1], lambda w: current[w, t + 1])
        return carry

    cell_row(0, lambda w: before[w], lambda w: current[w, 1])
    lax.fori_loop(1, cells - 1, step, 0)
    cell_row(cells - 1, lambda w: current[w, cells - 2], lambda w: after[w])
    if not last:
        for v in range(NVAR):
            rims[0][v] = out[v, 0]
            rims[1][v] = out[v, cells - 1]


def rim_shapes(current):
    nvar, cells, width, radial = current.shape
    theta_rim = jax.ShapeDtypeStruct((nvar, width, radial), jnp.float32)
    axial_rim = jax.ShapeDtypeStruct((nvar, cells, radial), jnp.float32)
    return (theta_rim, theta_rim, axial_rim, axial_rim)


def first_rims(place, current):
    return pl.pallas_call(
        rims_kernel,
        out_shape=rim_shapes(current),
        in_specs=[SMEM, VMEM],
        out_specs=(VMEM,) * 4,
        compiler_params=pltpu.CompilerParams(vmem_limit_bytes=8 << 20),
        name="rims",
    )(place, current)


def advance(section, blocks, last, place, flux, weights, current, conserved, ghosts):
    outs = (jax.ShapeDtypeStruct(current.shape, jnp.float32),)
    if not last:
        outs = outs + rim_shapes(current)
    nvar, cells, _, radial = current.shape
    return pl.pallas_call(
        functools.partial(section_kernel, section, blocks, last),
        out_shape=outs,
        in_specs=[SMEM, SMEM] + [VMEM] * 8,
        out_specs=(VMEM,) * len(outs),
        scratch_shapes=[pltpu.VMEM((nvar, cells, radial), jnp.float32)] * 2,
        compiler_params=pltpu.CompilerParams(vmem_limit_bytes=16 << 20),
        name="section",
    )(place, flux, weights, current, conserved, *ghosts)


def ring(by, sectors):
    return [(i, (i + by) % sectors) for i in range(sectors)]


def core_pairs(blocks):
    return [(a, a ^ 1) for a in range(blocks)]


FINE = 4


def spin_pairs(by, sectors, blocks):
    rotor, stator = blocks // 2 - 1, blocks // 2
    pairs = []
    for t in range(sectors):
        ahead = (t + by) % sectors
        pairs.append((t * blocks + rotor, ahead * blocks + rotor))
        pairs.append((ahead * blocks + stator, t * blocks + stator))
    return pairs


def hop_pairs(by, sectors, blocks):
    pairs = []
    for a in range(1, blocks - 1, 2):
        shift = by if a == blocks // 2 - 1 else 0
        for t in range(sectors):
            low, high = t * blocks + a, (t + shift) % sectors * blocks + a + 1
            pairs += [(low, high), (high, low)]
    return pairs


def exchange_hop(face, offset, at_plane, sectors, blocks):
    shifts = list(range(-1, FINE - 1))
    fine = (offset + 1) % FINE
    coarse = (offset + 1) // FINE % (sectors // FINE)

    def spin(by, value):
        if by == 0:
            return value
        moved = lax.ppermute(value, AXES, spin_pairs(by, sectors, blocks))
        return jnp.where(at_plane, moved, value)

    def hop(by, value):
        return lax.ppermute(value, AXES, hop_pairs(by, sectors, blocks))

    face = lax.switch(fine, [functools.partial(spin, by) for by in shifts], face)
    return lax.switch(
        coarse, [functools.partial(hop, FINE * k) for k in range(sectors // FINE)], face
    )


def local(conserved, flux_matrices, slide_weights, rotor_offsets):
    sectors, blocks = lax.axis_size("theta"), lax.axis_size("axial")
    index = lax.axis_index("axial")
    place = jnp.full((1,), index, jnp.int32)
    at_plane = (index == blocks // 2) | (index == blocks // 2 - 1)
    current, rims = conserved, first_rims(place, conserved)
    sections = len(SECTION_WEIGHTS)
    for section in range(sections):
        theta_low, theta_high, core_rim, hop_rim = rims
        before = lax.ppermute(theta_high, "theta", ring(1, sectors))
        after = lax.ppermute(theta_low, "theta", ring(-1, sectors))
        core_in = lax.ppermute(core_rim, "axial", core_pairs(blocks))
        hop_in = exchange_hop(hop_rim, rotor_offsets[section], at_plane, sectors, blocks)
        current, *rims = advance(
            section,
            blocks,
            section == sections - 1,
            place,
            flux_matrices,
            slide_weights,
            current,
            conserved,
            (before, after, core_in, hop_in, hop_rim),
        )
    return current


def solution(mesh):
    in_specs = (P(None, "theta", "axial", None), P(), P(), P())
    out_specs = P(None, "theta", "axial", None)
    return jax.shard_map(local, mesh=mesh, in_specs=in_specs, out_specs=out_specs, check_vma=False)
```

```python
import functools

import jax
import jax.numpy as jnp
from jax import lax
from jax.experimental import pallas as pl
from jax.experimental.pallas import tpu as pltpu
from jax.sharding import PartitionSpec as P

NVAR = 5
time_step = 0.25
viscosity = 0.3
SECTION_WEIGHTS = (
    (0.0, 1.0, time_step),
    (0.75, 0.25, 0.25 * time_step),
    (1.0 / 3.0, 2.0 / 3.0, 2.0 / 3.0 * time_step),
)
AXES = ("theta", "axial")
VMEM = pl.BlockSpec(memory_space=pltpu.VMEM)
SMEM = pl.BlockSpec(memory_space=pltpu.SMEM)


def write_axial_rims(value, v, t, is_odd, low_rim, high_rim, core_rim):
    first, last = value[:1], value[-1:]
    core_rim[v, pl.ds(t, 1), :] = jnp.where(is_odd, first, last)
    hop = jnp.where(is_odd, last, first)
    low_rim[NVAR + v, pl.ds(t, 1), :] = hop
    high_rim[NVAR + v, pl.ds(t, 1), :] = hop


def rims_kernel(place, current, low_rim, high_rim, core_rim):
    is_odd = place[0] % 2 == 1
    cells = current.shape[1]
    for v in range(NVAR):
        low_rim[v] = current[v, 0]
        high_rim[v] = current[v, cells - 1]

    def step(t, carry):
        for v in range(NVAR):
            write_axial_rims(current[v, t], v, t, is_odd, low_rim, high_rim, core_rim)
        return carry

    lax.fori_loop(0, cells, step, 0)


def section_kernel(section, blocks, last, *refs):
    place, flux, weights, current, conserved, before, after, core_in, hop_in, hop_own = refs[:10]
    rims = refs[11:-2]
    out, low_ghost, high_ghost = refs[10], refs[-2], refs[-1]
    index = place[0]
    is_odd = index % 2 == 1
    cells, width, radial = current.shape[1:]
    at_plane = (index == blocks // 2) | (index == blocks // 2 - 1)
    at_end = (index == 0) | (index == blocks - 1)
    inside = jnp.logical_not(at_plane | at_end)

    def put(core_side, hop_side):
        @pl.when(at_plane)
        def _():
            mix = weights[section, jnp.where(index == blocks // 2, 0, 1)]
            for v in range(NVAR):
                hop_side[v] = jnp.dot(
                    mix,
                    hop_in[v],
                    precision=lax.Precision.HIGHEST,
                    preferred_element_type=jnp.float32,
                )

        @pl.when(at_end)
        def _():
            hop_side[...] = hop_own[NVAR:]

        @pl.when(inside)
        def _():
            hop_side[...] = hop_in[...]

        core_side[...] = core_in[...]

    @pl.when(is_odd)
    def _():
        put(low_ghost, high_ghost)

    @pl.when(jnp.logical_not(is_odd))
    def _():
        put(high_ghost, low_ghost)

    keep, carry_on, push = SECTION_WEIGHTS[section]
    row = lax.broadcasted_iota(jnp.int32, (width, radial), 0)
    lane = lax.broadcasted_iota(jnp.int32, (width, radial), 1)

    def cell_row(t, minus_of, plus_of):
        slope = [None] * NVAR
        smooth = [None] * NVAR
        for w in range(NVAR):
            c = current[w, t]
            tm, tp = minus_of(w), plus_of(w)
            low = low_ghost[w, pl.ds(t, 1), :]
            high = high_ghost[w, pl.ds(t, 1), :]
            am = jnp.where(row == 0, low, pltpu.roll(c, 1, 0))
            ap = jnp.where(row == width - 1, high, pltpu.roll(c, width - 1, 0))
            rm = jnp.where(lane == 0, c, pltpu.roll(c, 1, 1))
            rp = jnp.where(lane == radial - 1, c, pltpu.roll(c, radial - 1, 1))
            total = (tm + tp) + (am + ap) + (rm + rp)
            smooth[w] = (viscosity * push) * total + (carry_on - 6.0 * viscosity * push) * c
            if section:
                smooth[w] = smooth[w] + keep * conserved[w, t]
            dt, da, dr = tp - tm, ap - am, rp - rm
            for v in range(NVAR):
                term = flux[0, v, w] * dt + flux[1, v, w] * da + flux[2, v, w] * dr
                slope[v] = term if slope[v] is None else slope[v] + term
        for v in range(NVAR):
            new = smooth[v] - (0.5 * push) * slope[v]
            out[v, t] = new
            if not last:
                write_axial_rims(new, v, t, is_odd, *rims)

    def step(t, carry):
        cell_row(t, lambda w: current[w, t - 1], lambda w: current[w, t + 1])
        return carry

    cell_row(0, lambda w: before[w], lambda w: current[w, 1])
    lax.fori_loop(1, cells - 1, step, 0)
    cell_row(cells - 1, lambda w: current[w, cells - 2], lambda w: after[w])
    if not last:
        for v in range(NVAR):
            rims[0][v] = out[v, 0]
            rims[1][v] = out[v, cells - 1]


def rim_shapes(current):
    nvar, cells, width, radial = current.shape
    theta_rim = jax.ShapeDtypeStruct((2 * nvar, width, radial), jnp.float32)
    axial_rim = jax.ShapeDtypeStruct((nvar, cells, radial), jnp.float32)
    return (theta_rim, theta_rim, axial_rim)


def first_rims(place, current):
    return pl.pallas_call(
        rims_kernel,
        out_shape=rim_shapes(current),
        in_specs=[SMEM, VMEM],
        out_specs=(VMEM,) * 3,
        compiler_params=pltpu.CompilerParams(vmem_limit_bytes=8 << 20),
        name="rims",
    )(place, current)


def advance(section, blocks, last, place, flux, weights, current, conserved, ghosts):
    outs = (jax.ShapeDtypeStruct(current.shape, jnp.float32),)
    if not last:
        outs = outs + rim_shapes(current)
    nvar, cells, _, radial = current.shape
    return pl.pallas_call(
        functools.partial(section_kernel, section, blocks, last),
        out_shape=outs,
        in_specs=[SMEM, SMEM] + [VMEM] * 8,
        out_specs=(VMEM,) * len(outs),
        scratch_shapes=[pltpu.VMEM((nvar, cells, radial), jnp.float32)] * 2,
        compiler_params=pltpu.CompilerParams(vmem_limit_bytes=16 << 20),
        name="section",
    )(place, flux, weights, current, conserved, *ghosts)


def ring(by, sectors):
    return [(i, (i + by) % sectors) for i in range(sectors)]


def core_pairs(blocks):
    return [(a, a ^ 1) for a in range(blocks)]


def hop_pairs(by, sectors, blocks):
    pairs = []
    for a in range(1, blocks - 1, 2):
        shift = by if a == blocks // 2 - 1 else 0
        for t in range(sectors):
            low, high = t * blocks + a, (t + shift) % sectors * blocks + a + 1
            pairs += [(low, high), (high, low)]
    return pairs


def exchange_hop(own, before, after, offset, side, sectors, blocks):
    fine = (offset + 1) % 3 - 1
    coarse = (offset + 1) // 3 % (sectors // 3)
    turn = fine * side
    face = jnp.where(turn == 1, before, jnp.where(turn == -1, after, own))

    def hop(by, value):
        return lax.ppermute(value, AXES, hop_pairs(by, sectors, blocks))

    return lax.switch(coarse, [functools.partial(hop, 3 * k) for k in range(sectors // 3)], face)


def local(conserved, flux_matrices, slide_weights, rotor_offsets):
    sectors, blocks = lax.axis_size("theta"), lax.axis_size("axial")
    index = lax.axis_index("axial")
    place = jnp.full((1,), index, jnp.int32)
    side = jnp.where(index == blocks // 2 - 1, 1, jnp.where(index == blocks // 2, -1, 0))
    current, rims = conserved, first_rims(place, conserved)
    sections = len(SECTION_WEIGHTS)
    for section in range(sections):
        low_rim, high_rim, core_rim = rims
        before = lax.ppermute(high_rim, "theta", ring(1, sectors))
        after = lax.ppermute(low_rim, "theta", ring(-1, sectors))
        core_in = lax.ppermute(core_rim, "axial", core_pairs(blocks))
        hop_in = exchange_hop(
            low_rim[NVAR:],
            before[NVAR:],
            after[NVAR:],
            rotor_offsets[section],
            side,
            sectors,
            blocks,
        )
        current, *rims = advance(
            section,
            blocks,
            section == sections - 1,
            place,
            flux_matrices,
            slide_weights,
            current,
            conserved,
            (before, after, core_in, hop_in, low_rim),
        )
    return current


def solution(mesh):
    in_specs = (P(None, "theta", "axial", None), P(), P(), P())
    out_specs = P(None, "theta", "axial", None)
    return jax.shard_map(local, mesh=mesh, in_specs=in_specs, out_specs=out_specs, check_vma=False)
```

```python
import functools

import jax
import jax.numpy as jnp
from jax import lax
from jax.experimental import pallas as pl
from jax.experimental.pallas import tpu as pltpu
from jax.sharding import PartitionSpec as P

NVAR = 5
time_step = 0.25
viscosity = 0.3
SECTION_WEIGHTS = (
    (0.0, 1.0, time_step),
    (0.75, 0.25, 0.25 * time_step),
    (1.0 / 3.0, 2.0 / 3.0, 2.0 / 3.0 * time_step),
)
AXES = ("theta", "axial")
VMEM = pl.BlockSpec(memory_space=pltpu.VMEM)
SMEM = pl.BlockSpec(memory_space=pltpu.SMEM)


def write_axial_rims(value, v, t, is_odd, low_rim, high_rim, core_rim):
    first, last = value[:1], value[-1:]
    core_rim[v, pl.ds(t, 1), :] = jnp.where(is_odd, first, last)
    hop = jnp.where(is_odd, last, first)
    low_rim[NVAR + v, pl.ds(t, 1), :] = hop
    high_rim[NVAR + v, pl.ds(t, 1), :] = hop


def rims_kernel(place, current, low_rim, high_rim, core_rim):
    is_odd = lax.rem(place[0], 2) == 1
    cells = current.shape[1]
    for v in range(NVAR):
        low_rim[v] = current[v, 0]
        high_rim[v] = current[v, cells - 1]

    def step(t, carry):
        for v in range(NVAR):
            write_axial_rims(current[v, t], v, t, is_odd, low_rim, high_rim, core_rim)
        return carry

    lax.fori_loop(0, cells, step, 0)


def section_kernel(section, blocks, last, *refs):
    place, flux, weights, current, conserved, before, after, core_in, hop_in, hop_own = refs[:10]
    rims = refs[11:-2]
    out, low_ghost, high_ghost = refs[10], refs[-2], refs[-1]
    index = lax.rem(place[0], blocks)
    is_odd = lax.rem(index, 2) == 1
    cells, width, radial = current.shape[1:]
    at_plane = (index == blocks // 2) | (index == blocks // 2 - 1)
    at_end = (index == 0) | (index == blocks - 1)
    inside = jnp.logical_not(at_plane | at_end)

    def put(core_side, hop_side):
        @pl.when(at_plane)
        def _():
            mix = weights[section, jnp.where(index == blocks // 2, 0, 1)]
            for v in range(NVAR):
                hop_side[v] = jnp.dot(
                    mix,
                    hop_in[v],
                    precision=lax.Precision.HIGHEST,
                    preferred_element_type=jnp.float32,
                )

        @pl.when(at_end)
        def _():
            hop_side[...] = hop_own[NVAR:]

        @pl.when(inside)
        def _():
            hop_side[...] = hop_in[...]

        core_side[...] = core_in[...]

    @pl.when(is_odd)
    def _():
        put(low_ghost, high_ghost)

    @pl.when(jnp.logical_not(is_odd))
    def _():
        put(high_ghost, low_ghost)

    keep, carry_on, push = SECTION_WEIGHTS[section]
    row = lax.broadcasted_iota(jnp.int32, (width, radial), 0)
    lane = lax.broadcasted_iota(jnp.int32, (width, radial), 1)

    def cell_row(t, minus_of, plus_of):
        slope = [None] * NVAR
        smooth = [None] * NVAR
        for w in range(NVAR):
            c = current[w, t]
            tm, tp = minus_of(w), plus_of(w)
            low = low_ghost[w, pl.ds(t, 1), :]
            high = high_ghost[w, pl.ds(t, 1), :]
            am = jnp.where(row == 0, low, pltpu.roll(c, 1, 0))
            ap = jnp.where(row == width - 1, high, pltpu.roll(c, width - 1, 0))
            rm = jnp.where(lane == 0, c, pltpu.roll(c, 1, 1))
            rp = jnp.where(lane == radial - 1, c, pltpu.roll(c, radial - 1, 1))
            total = (tm + tp) + (am + ap) + (rm + rp)
            smooth[w] = (viscosity * push) * total + (carry_on - 6.0 * viscosity * push) * c
            if section:
                smooth[w] = smooth[w] + keep * conserved[w, t]
            dt, da, dr = tp - tm, ap - am, rp - rm
            for v in range(NVAR):
                term = flux[v, 0, w] * dt + flux[v, 1, w] * da + flux[v, 2, w] * dr
                slope[v] = term if slope[v] is None else slope[v] + term
        for v in range(NVAR):
            new = smooth[v] - (0.5 * push) * slope[v]
            out[v, t] = new
            if not last:
                write_axial_rims(new, v, t, is_odd, *rims)

    def step(t, carry):
        cell_row(t, lambda w: current[w, t - 1], lambda w: current[w, t + 1])
        return carry

    cell_row(0, lambda w: before[w], lambda w: current[w, 1])
    lax.fori_loop(1, cells - 1, step, 0, unroll=2)
    cell_row(cells - 1, lambda w: current[w, cells - 2], lambda w: after[w])
    if not last:
        for v in range(NVAR):
            rims[0][v] = out[v, 0]
            rims[1][v] = out[v, cells - 1]


def rim_shapes(current):
    nvar, cells, width, radial = current.shape
    theta_rim = jax.ShapeDtypeStruct((2 * nvar, width, radial), jnp.float32)
    axial_rim = jax.ShapeDtypeStruct((nvar, cells, radial), jnp.float32)
    return (theta_rim, theta_rim, axial_rim)


def first_rims(place, current):
    return pl.pallas_call(
        rims_kernel,
        out_shape=rim_shapes(current),
        in_specs=[SMEM, VMEM],
        out_specs=(VMEM,) * 3,
        compiler_params=pltpu.CompilerParams(vmem_limit_bytes=8 << 20),
        name="rims",
    )(place, current)


def advance(section, blocks, last, place, flux, weights, current, conserved, ghosts):
    outs = (jax.ShapeDtypeStruct(current.shape, jnp.float32),)
    if not last:
        outs = outs + rim_shapes(current)
    nvar, cells, _, radial = current.shape
    return pl.pallas_call(
        functools.partial(section_kernel, section, blocks, last),
        out_shape=outs,
        in_specs=[SMEM, SMEM] + [VMEM] * 8,
        out_specs=(VMEM,) * len(outs),
        scratch_shapes=[pltpu.VMEM((nvar, cells, radial), jnp.float32)] * 2,
        compiler_params=pltpu.CompilerParams(vmem_limit_bytes=16 << 20),
        name="section",
    )(place, flux, weights, current, conserved, *ghosts)


def ring(by, sectors):
    return [(i, (i + by) % sectors) for i in range(sectors)]


def core_pairs(blocks):
    return [(a, a ^ 1) for a in range(blocks)]


def hop_pairs(by, sectors, blocks):
    pairs = []
    for a in range(1, blocks - 1, 2):
        shift = by if a == blocks // 2 - 1 else 0
        for t in range(sectors):
            low, high = t * blocks + a, (t + shift) % sectors * blocks + a + 1
            pairs += [(low, high), (high, low)]
    return pairs


def exchange_hop(own, before, after, offset, index, sectors, blocks):
    moved = offset + 1
    thirds = (moved * 171) >> 9
    coarse = jnp.where(thirds == sectors // 3, 0, thirds)
    fine = moved - 3 * thirds
    rotor, stator = index == blocks // 2 - 1, index == blocks // 2
    take_before = ((fine == 2) & rotor) | ((fine == 0) & stator)
    take_after = ((fine == 0) & rotor) | ((fine == 2) & stator)
    face = jnp.where(take_before, before, jnp.where(take_after, after, own))

    def hop(by, value):
        return lax.ppermute(value, AXES, hop_pairs(by, sectors, blocks))

    return lax.switch(coarse, [functools.partial(hop, 3 * k) for k in range(sectors // 3)], face)


def local(conserved, flux_matrices, slide_weights, rotor_offsets):
    sectors, blocks = lax.axis_size("theta"), lax.axis_size("axial")
    index = lax.axis_index("axial")
    place = jnp.full((1,), lax.axis_index("theta") * blocks + index, jnp.int32)
    flux = jnp.transpose(flux_matrices, (1, 0, 2))
    current, rims = conserved, first_rims(place, conserved)
    sections = len(SECTION_WEIGHTS)
    for section in range(sections):
        low_rim, high_rim, core_rim = rims
        before = lax.ppermute(high_rim, "theta", ring(1, sectors))
        after = lax.ppermute(low_rim, "theta", ring(-1, sectors))
        core_in = lax.ppermute(core_rim, "axial", core_pairs(blocks))
        hop_in = exchange_hop(
            low_rim[NVAR:],
            before[NVAR:],
            after[NVAR:],
            rotor_offsets[section],
            index,
            sectors,
            blocks,
        )
        current, *rims = advance(
            section,
            blocks,
            section == sections - 1,
            place,
            flux,
            slide_weights,
            current,
            conserved,
            (before, after, core_in, hop_in, low_rim),
        )
    return current


def solution(mesh):
    in_specs = (P(None, "theta", "axial", None), P(), P(), P())
    out_specs = P(None, "theta", "axial", None)
    return jax.shard_map(local, mesh=mesh, in_specs=in_specs, out_specs=out_specs, check_vma=False)
```

```python
import functools

import jax
import jax.numpy as jnp
from jax import lax
from jax.experimental import pallas as pl
from jax.experimental.pallas import tpu as pltpu
from jax.sharding import PartitionSpec as P

NVAR = 5
time_step = 0.25
viscosity = 0.3
SECTION_WEIGHTS = (
    (0.0, 1.0, time_step),
    (0.75, 0.25, 0.25 * time_step),
    (1.0 / 3.0, 2.0 / 3.0, 2.0 / 3.0 * time_step),
)
AXES = ("theta", "axial")
VMEM = pl.BlockSpec(memory_space=pltpu.VMEM)
SMEM = pl.BlockSpec(memory_space=pltpu.SMEM)


def write_axial_rims(value, v, t, is_odd, low_rim, high_rim, core_rim):
    first, last = value[:1], value[-1:]
    core_rim[v, pl.ds(t, 1), :] = jnp.where(is_odd, first, last)
    hop = jnp.where(is_odd, last, first)
    low_rim[NVAR + v, pl.ds(t, 1), :] = hop
    high_rim[NVAR + v, pl.ds(t, 1), :] = hop


def rims_kernel(place, current, low_rim, high_rim, core_rim):
    is_odd = lax.rem(place[0], 2) == 1
    cells = current.shape[1]
    for v in range(NVAR):
        low_rim[v] = current[v, 0]
        high_rim[v] = current[v, cells - 1]

    def step(t, carry):
        for v in range(NVAR):
            write_axial_rims(current[v, t], v, t, is_odd, low_rim, high_rim, core_rim)
        return carry

    lax.fori_loop(0, cells, step, 0)


def section_kernel(section, blocks, last, *refs):
    place, flux, weights, current, conserved, before, after, core_in, hop_in, hop_own = refs[:10]
    rims = refs[11:-2]
    out, low_ghost, high_ghost = refs[10], refs[-2], refs[-1]
    index = lax.rem(place[0], blocks)
    is_odd = lax.rem(index, 2) == 1
    cells, width, radial = current.shape[1:]
    at_plane = (index == blocks // 2) | (index == blocks // 2 - 1)
    at_end = (index == 0) | (index == blocks - 1)
    inside = jnp.logical_not(at_plane | at_end)

    def put(core_side, hop_side):
        @pl.when(at_plane)
        def _():
            mix = weights[section, jnp.where(index == blocks // 2, 0, 1)]
            for v in range(NVAR):
                hop_side[v] = jnp.dot(
                    mix,
                    hop_in[v],
                    precision=lax.Precision.HIGHEST,
                    preferred_element_type=jnp.float32,
                )

        @pl.when(at_end)
        def _():
            hop_side[...] = hop_own[NVAR:]

        @pl.when(inside)
        def _():
            hop_side[...] = hop_in[...]

        core_side[...] = core_in[...]

    @pl.when(is_odd)
    def _():
        put(low_ghost, high_ghost)

    @pl.when(jnp.logical_not(is_odd))
    def _():
        put(high_ghost, low_ghost)

    keep, carry_on, push = SECTION_WEIGHTS[section]
    row = lax.broadcasted_iota(jnp.int32, (width, radial), 0)
    lane = lax.broadcasted_iota(jnp.int32, (width, radial), 1)

    def cell_row(t, minus_of, plus_of):
        slope = [None] * NVAR
        smooth = [None] * NVAR
        for w in range(NVAR):
            c = current[w, t]
            tm, tp = minus_of(w), plus_of(w)
            low = low_ghost[w, pl.ds(t, 1), :]
            high = high_ghost[w, pl.ds(t, 1), :]
            am = jnp.where(row == 0, low, pltpu.roll(c, 1, 0))
            ap = jnp.where(row == width - 1, high, pltpu.roll(c, width - 1, 0))
            rm = jnp.where(lane == 0, c, pltpu.roll(c, 1, 1))
            rp = jnp.where(lane == radial - 1, c, pltpu.roll(c, radial - 1, 1))
            total = (tm + tp) + (am + ap) + (rm + rp)
            smooth[w] = (viscosity * push) * total + (carry_on - 6.0 * viscosity * push) * c
            if section:
                smooth[w] = smooth[w] + keep * conserved[w, t]
            dt, da, dr = tp - tm, ap - am, rp - rm
            for v in range(NVAR):
                term = flux[v, 0, w] * dt + flux[v, 1, w] * da + flux[v, 2, w] * dr
                slope[v] = term if slope[v] is None else slope[v] + term
        for v in range(NVAR):
            new = smooth[v] - (0.5 * push) * slope[v]
            out[v, t] = new
            if not last:
                write_axial_rims(new, v, t, is_odd, *rims)

    def step(t, carry):
        cell_row(t, lambda w: current[w, t - 1], lambda w: current[w, t + 1])
        return carry

    cell_row(0, lambda w: before[w], lambda w: current[w, 1])
    cell_row(cells - 1, lambda w: current[w, cells - 2], lambda w: after[w])
    lax.fori_loop(1, cells - 1, step, 0, unroll=2)
    if not last:
        for v in range(NVAR):
            rims[0][v] = out[v, 0]
            rims[1][v] = out[v, cells - 1]


def rim_shapes(current):
    nvar, cells, width, radial = current.shape
    theta_rim = jax.ShapeDtypeStruct((2 * nvar, width, radial), jnp.float32)
    axial_rim = jax.ShapeDtypeStruct((nvar, cells, radial), jnp.float32)
    return (theta_rim, theta_rim, axial_rim)


def first_rims(place, current):
    return pl.pallas_call(
        rims_kernel,
        out_shape=rim_shapes(current),
        in_specs=[SMEM, VMEM],
        out_specs=(VMEM,) * 3,
        compiler_params=pltpu.CompilerParams(vmem_limit_bytes=8 << 20),
        name="rims",
    )(place, current)


def advance(section, blocks, last, place, flux, weights, current, conserved, ghosts):
    outs = (jax.ShapeDtypeStruct(current.shape, jnp.float32),)
    if not last:
        outs = outs + rim_shapes(current)
    nvar, cells, _, radial = current.shape
    return pl.pallas_call(
        functools.partial(section_kernel, section, blocks, last),
        out_shape=outs,
        in_specs=[SMEM, SMEM] + [VMEM] * 8,
        out_specs=(VMEM,) * len(outs),
        scratch_shapes=[pltpu.VMEM((nvar, cells, radial), jnp.float32)] * 2,
        compiler_params=pltpu.CompilerParams(vmem_limit_bytes=16 << 20),
        name="section",
    )(place, flux, weights, current, conserved, *ghosts)


def ring(by, sectors):
    return [(i, (i + by) % sectors) for i in range(sectors)]


def core_pairs(blocks):
    return [(a, a ^ 1) for a in range(blocks)]


def hop_pairs(by, sectors, blocks):
    pairs = []
    for a in range(1, blocks - 1, 2):
        shift = by if a == blocks // 2 - 1 else 0
        for t in range(sectors):
            low, high = t * blocks + a, (t + shift) % sectors * blocks + a + 1
            pairs += [(low, high), (high, low)]
    return pairs


def exchange_hop(own, before, after, offset, index, sectors, blocks):
    moved = offset + 1
    thirds = (moved * 171) >> 9
    coarse = jnp.where(thirds == sectors // 3, 0, thirds)
    fine = moved - 3 * thirds
    rotor, stator = index == blocks // 2 - 1, index == blocks // 2
    take_before = ((fine == 2) & rotor) | ((fine == 0) & stator)
    take_after = ((fine == 0) & rotor) | ((fine == 2) & stator)
    face = jnp.where(take_before, before, jnp.where(take_after, after, own))

    def hop(by, value):
        return lax.ppermute(value, AXES, hop_pairs(by, sectors, blocks))

    return lax.switch(coarse, [functools.partial(hop, 3 * k) for k in range(sectors // 3)], face)


def local(conserved, flux_matrices, slide_weights, rotor_offsets):
    sectors, blocks = lax.axis_size("theta"), lax.axis_size("axial")
    index = lax.axis_index("axial")
    place = jnp.full((1,), lax.axis_index("theta") * blocks + index, jnp.int32)
    flux = jnp.transpose(flux_matrices, (1, 0, 2))
    current, rims = conserved, first_rims(place, conserved)
    sections = len(SECTION_WEIGHTS)
    for section in range(sections):
        low_rim, high_rim, core_rim = rims
        before = lax.ppermute(high_rim, "theta", ring(1, sectors))
        after = lax.ppermute(low_rim, "theta", ring(-1, sectors))
        core_in = lax.ppermute(core_rim, "axial", core_pairs(blocks))
        hop_in = exchange_hop(
            low_rim[NVAR:],
            before[NVAR:],
            after[NVAR:],
            rotor_offsets[section],
            index,
            sectors,
            blocks,
        )
        current, *rims = advance(
            section,
            blocks,
            section == sections - 1,
            place,
            flux,
            slide_weights,
            current,
            conserved,
            (before, after, core_in, hop_in, low_rim),
        )
    return current


def solution(mesh):
    in_specs = (P(None, "theta", "axial", None), P(), P(), P())
    out_specs = P(None, "theta", "axial", None)
    return jax.shard_map(local, mesh=mesh, in_specs=in_specs, out_specs=out_specs, check_vma=False)
```

```python
import functools

import jax
import jax.numpy as jnp
from jax import lax
from jax.experimental import pallas as pl
from jax.experimental.pallas import tpu as pltpu
from jax.sharding import PartitionSpec as P

NVAR = 5
time_step = 0.25
viscosity = 0.3
SECTION_WEIGHTS = (
    (0.0, 1.0, time_step),
    (0.75, 0.25, 0.25 * time_step),
    (1.0 / 3.0, 2.0 / 3.0, 2.0 / 3.0 * time_step),
)
AXES = ("theta", "axial")
VMEM = pl.BlockSpec(memory_space=pltpu.VMEM)
SMEM = pl.BlockSpec(memory_space=pltpu.SMEM)


def write_axial_rims(value, v, t, is_odd, low_rim, high_rim, core_rim):
    first, last = value[:1], value[-1:]
    core_rim[v, pl.ds(t, 1), :] = jnp.where(is_odd, first, last)
    hop = jnp.where(is_odd, last, first)
    low_rim[NVAR + v, pl.ds(t, 1), :] = hop
    high_rim[NVAR + v, pl.ds(t, 1), :] = hop


def rims_kernel(place, current, low_rim, high_rim, core_rim):
    is_odd = lax.rem(place[0], 2) == 1
    cells = current.shape[1]
    for v in range(NVAR):
        low_rim[v] = current[v, 0]
        high_rim[v] = current[v, cells - 1]

    def step(t, carry):
        for v in range(NVAR):
            write_axial_rims(current[v, t], v, t, is_odd, low_rim, high_rim, core_rim)
        return carry

    lax.fori_loop(0, cells, step, 0)


def section_kernel(section, blocks, last, *refs):
    place, flux, weights, current, conserved, before, after, core_in, hop_in, hop_own = refs[:10]
    if last:
        whole, low_ghost, high_ghost, out, sems = refs[10:]
        rims = ()
    else:
        rims = refs[11:-2]
        out, low_ghost, high_ghost = refs[10], refs[-2], refs[-1]
    index = lax.rem(place[0], blocks)
    is_odd = lax.rem(index, 2) == 1
    cells, width, radial = current.shape[1:]
    at_plane = (index == blocks // 2) | (index == blocks // 2 - 1)
    at_end = (index == 0) | (index == blocks - 1)
    inside = jnp.logical_not(at_plane | at_end)

    def put(core_side, hop_side):
        @pl.when(at_plane)
        def _():
            mix = weights[section, jnp.where(index == blocks // 2, 0, 1)]
            for v in range(NVAR):
                hop_side[v] = jnp.dot(
                    mix,
                    hop_in[v],
                    precision=lax.Precision.HIGHEST,
                    preferred_element_type=jnp.float32,
                )

        @pl.when(at_end)
        def _():
            hop_side[...] = hop_own[NVAR:]

        @pl.when(inside)
        def _():
            hop_side[...] = hop_in[...]

        core_side[...] = core_in[...]

    @pl.when(is_odd)
    def _():
        put(low_ghost, high_ghost)

    @pl.when(jnp.logical_not(is_odd))
    def _():
        put(high_ghost, low_ghost)

    keep, carry_on, push = SECTION_WEIGHTS[section]
    row = lax.broadcasted_iota(jnp.int32, (width, radial), 0)
    lane = lax.broadcasted_iota(jnp.int32, (width, radial), 1)

    def cell_row(t, minus_of, plus_of):
        slope = [None] * NVAR
        smooth = [None] * NVAR
        for w in range(NVAR):
            c = current[w, t]
            tm, tp = minus_of(w), plus_of(w)
            low = low_ghost[w, pl.ds(t, 1), :]
            high = high_ghost[w, pl.ds(t, 1), :]
            am = jnp.where(row == 0, low, pltpu.roll(c, 1, 0))
            ap = jnp.where(row == width - 1, high, pltpu.roll(c, width - 1, 0))
            rm = jnp.where(lane == 0, c, pltpu.roll(c, 1, 1))
            rp = jnp.where(lane == radial - 1, c, pltpu.roll(c, radial - 1, 1))
            total = (tm + tp) + (am + ap) + (rm + rp)
            smooth[w] = (viscosity * push) * total + (carry_on - 6.0 * viscosity * push) * c
            if section:
                smooth[w] = smooth[w] + keep * conserved[w, t]
            dt, da, dr = tp - tm, ap - am, rp - rm
            for v in range(NVAR):
                term = flux[v, 0, w] * dt + flux[v, 1, w] * da + flux[v, 2, w] * dr
                slope[v] = term if slope[v] is None else slope[v] + term
        for v in range(NVAR):
            new = smooth[v] - (0.5 * push) * slope[v]
            out[v, t] = new
            if not last:
                write_axial_rims(new, v, t, is_odd, *rims)

    def step(t, carry):
        cell_row(t, lambda w: current[w, t - 1], lambda w: current[w, t + 1])
        return carry

    cell_row(0, lambda w: before[w], lambda w: current[w, 1])
    cell_row(cells - 1, lambda w: current[w, cells - 2], lambda w: after[w])
    if last:
        cut = 7
        head = pltpu.make_async_copy(out.at[:, :cut], whole.at[:, :cut], sems.at[0])
        tail = pltpu.make_async_copy(out.at[:, cut:], whole.at[:, cut:], sems.at[1])
        lax.fori_loop(1, cut, step, 0, unroll=2)
        head.start()
        lax.fori_loop(cut, cells - 1, step, 0, unroll=2)
        tail.start()
        head.wait()
        tail.wait()
        return
    lax.fori_loop(1, cells - 1, step, 0, unroll=2)
    if not last:
        for v in range(NVAR):
            rims[0][v] = out[v, 0]
            rims[1][v] = out[v, cells - 1]


def rim_shapes(current):
    nvar, cells, width, radial = current.shape
    theta_rim = jax.ShapeDtypeStruct((2 * nvar, width, radial), jnp.float32)
    axial_rim = jax.ShapeDtypeStruct((nvar, cells, radial), jnp.float32)
    return (theta_rim, theta_rim, axial_rim)


def first_rims(place, current):
    return pl.pallas_call(
        rims_kernel,
        out_shape=rim_shapes(current),
        in_specs=[SMEM, VMEM],
        out_specs=(VMEM,) * 3,
        compiler_params=pltpu.CompilerParams(vmem_limit_bytes=8 << 20),
        name="rims",
    )(place, current)


def advance(section, blocks, last, place, flux, weights, current, conserved, ghosts):
    outs = (jax.ShapeDtypeStruct(current.shape, jnp.float32),)
    if not last:
        outs = outs + rim_shapes(current)
    nvar, cells, _, radial = current.shape
    scratch = [pltpu.VMEM((nvar, cells, radial), jnp.float32)] * 2
    if last:
        scratch += [pltpu.VMEM(current.shape, jnp.float32), pltpu.SemaphoreType.DMA((2,))]
    return pl.pallas_call(
        functools.partial(section_kernel, section, blocks, last),
        out_shape=outs,
        in_specs=[SMEM, SMEM] + [VMEM] * 8,
        out_specs=(pl.BlockSpec(memory_space=pl.ANY),) if last else (VMEM,) * len(outs),
        scratch_shapes=scratch,
        compiler_params=pltpu.CompilerParams(vmem_limit_bytes=16 << 20),
        name="section",
    )(place, flux, weights, current, conserved, *ghosts)


def ring(by, sectors):
    return [(i, (i + by) % sectors) for i in range(sectors)]


def core_pairs(blocks):
    return [(a, a ^ 1) for a in range(blocks)]


def hop_pairs(by, sectors, blocks):
    pairs = []
    for a in range(1, blocks - 1, 2):
        shift = by if a == blocks // 2 - 1 else 0
        for t in range(sectors):
            low, high = t * blocks + a, (t + shift) % sectors * blocks + a + 1
            pairs += [(low, high), (high, low)]
    return pairs


def exchange_hop(own, before, after, offset, index, sectors, blocks):
    moved = offset + 1
    thirds = (moved * 171) >> 9
    coarse = jnp.where(thirds == sectors // 3, 0, thirds)
    fine = moved - 3 * thirds
    rotor, stator = index == blocks // 2 - 1, index == blocks // 2
    take_before = ((fine == 2) & rotor) | ((fine == 0) & stator)
    take_after = ((fine == 0) & rotor) | ((fine == 2) & stator)
    face = jnp.where(take_before, before, jnp.where(take_after, after, own))

    def hop(by, value):
        return lax.ppermute(value, AXES, hop_pairs(by, sectors, blocks))

    return lax.switch(coarse, [functools.partial(hop, 3 * k) for k in range(sectors // 3)], face)


def local(conserved, flux_matrices, slide_weights, rotor_offsets):
    sectors, blocks = lax.axis_size("theta"), lax.axis_size("axial")
    index = lax.axis_index("axial")
    place = jnp.full((1,), lax.axis_index("theta") * blocks + index, jnp.int32)
    flux = jnp.transpose(flux_matrices, (1, 0, 2))
    current, rims = conserved, first_rims(place, conserved)
    sections = len(SECTION_WEIGHTS)
    for section in range(sections):
        low_rim, high_rim, core_rim = rims
        before = lax.ppermute(high_rim, "theta", ring(1, sectors))
        after = lax.ppermute(low_rim, "theta", ring(-1, sectors))
        core_in = lax.ppermute(core_rim, "axial", core_pairs(blocks))
        hop_in = exchange_hop(
            low_rim[NVAR:],
            before[NVAR:],
            after[NVAR:],
            rotor_offsets[section],
            index,
            sectors,
            blocks,
        )
        current, *rims = advance(
            section,
            blocks,
            section == sections - 1,
            place,
            flux,
            slide_weights,
            current,
            conserved,
            (before, after, core_in, hop_in, low_rim),
        )
    return current


def solution(mesh):
    in_specs = (P(None, "theta", "axial", None), P(), P(), P())
    out_specs = P(None, "theta", "axial", None)
    return jax.shard_map(local, mesh=mesh, in_specs=in_specs, out_specs=out_specs, check_vma=False)
```
